32 devices in a mesh: pipe: 4 (over y, x), fsdp: 8 (over z, core).
Axes of the slice: x: 2, y: 2, z: 4, core: 2. Of those that a mesh axis runs over, the one named last changes fastest.
Arguments:
- tokens: bfloat16 [512, 12288], P(None, 'pipe'), may hold values from -6 to 6
- cotangent: bfloat16 [512, 12288], P(None, 'pipe'), may hold values from -6 to 6
- gate_weight: bfloat16 [12288, 28672], P('pipe', 'fsdp'), may hold values from -0.0546875 to 0.0546875
- up_weight: bfloat16 [12288, 28672], P('pipe', 'fsdp'), may hold values from -0.0546875 to 0.0546875
- down_weight: bfloat16 [28672, 12288], P('fsdp', 'pipe'), may hold values from -0.0546875 to 0.0546875
- adapter_down_first: bfloat16 [28672, 64], P('fsdp'), may hold values from -0.03125 to 0.03125
- adapter_down_second: bfloat16 [64, 12288], P(None, 'pipe'), may hold values from -0.29882812 to 0.29882812
Outputs:
- grad_input: bfloat16 [512, 12288], P('fsdp', 'pipe')
- grad_lora_a: float32 [28672, 64], P('fsdp')
- grad_lora_b: float32 [64, 12288], P(None, 'pipe')
The draws below stay inside these ranges and needn't reach their ends.
All inputs are finite; a program needn't handle non-finite values.
Results may differ from the reference program's by a relative error of at most 0.005.
Values may be sent and summed in bfloat16 or wider, within the bound.
No kernel may reach another device: no remote copies, remote signals or barrier semaphores. Data moves between devices by JAX's collectives and lax.ppermute only.
A program may use at most 192 MiB of HBM per device.

```python
import jax
import jax.numpy as jnp

MODEL_WIDTH = 12288
HIDDEN_UNITS = 28672
ADAPTER_RANK = 64
TOKENS = 512


def block_levels(stream_key, dims, cuts, least, top_value):
    gain = 1.0
    for dim, parts in cuts:
        steps = jax.random.uniform(jax.random.fold_in(jax.random.fold_in(stream_key, 6), dim), (parts,), jnp.float32, least / len(cuts), top_value / len(cuts))
        gain = gain * jnp.repeat(jnp.exp(steps), dims[dim] // parts).reshape((-1,) + (1,) * (len(dims) - 1 - dim))
    return gain


def normal_values(rng, dims, deviation, limit, split=(), dtype=jnp.bfloat16):
    entries = deviation * jax.random.normal(rng, dims, jnp.float32)
    if split:
        entries = entries * block_levels(rng, dims, split, -0.22, 0.18)
    return jnp.clip(entries, -limit, limit).astype(dtype)


def setup_inputs(seed: int = 0) -> dict:
    arg_keys = jax.random.split(jax.random.key(seed), 8)
    tokens = normal_values(arg_keys[0], (TOKENS, MODEL_WIDTH), 1.0, 6.0, ((1, 4),))
    cotangent = normal_values(arg_keys[1], (TOKENS, MODEL_WIDTH), 1.0, 6.0, ((1, 4),))
    gate_weight = normal_values(arg_keys[2], (MODEL_WIDTH, HIDDEN_UNITS), MODEL_WIDTH ** -0.5, 0.0546875, ((0, 4), (1, 8)))
    up_weight = normal_values(arg_keys[3], (MODEL_WIDTH, HIDDEN_UNITS), MODEL_WIDTH ** -0.5, 0.0546875, ((0, 4), (1, 8)))
    down_weight = normal_values(arg_keys[4], (HIDDEN_UNITS, MODEL_WIDTH), MODEL_WIDTH ** -0.5, 0.0546875, ((0, 8), (1, 4)))
    adapter_down_first = normal_values(arg_keys[5], (HIDDEN_UNITS, ADAPTER_RANK), HIDDEN_UNITS ** -0.5, 0.03125, ((0, 8),))
    adapter_down_second = normal_values(arg_keys[6], (ADAPTER_RANK, MODEL_WIDTH), 0.05, 0.29882812, ((1, 4),))
    return {"tokens": tokens, "cotangent": cotangent, "gate_weight": gate_weight, "up_weight": up_weight, "down_weight": down_weight, "adapter_down_first": adapter_down_first, "adapter_down_second": adapter_down_second}


adapter_scale = 0.5


def reference(tokens, cotangent, gate_weight, up_weight, down_weight, adapter_down_first, adapter_down_second):
    gate = jnp.dot(tokens, gate_weight, preferred_element_type=jnp.float32)
    up_values = jnp.dot(tokens, up_weight, preferred_element_type=jnp.float32)
    sigmoid_gate = jax.nn.sigmoid(gate)
    silu_gate = gate * sigmoid_gate
    hidden_activation = (silu_gate * up_values).astype(jnp.bfloat16)
    lowrank_product = jnp.dot(hidden_activation, adapter_down_first, preferred_element_type=jnp.float32).astype(jnp.bfloat16)
    backward_lowrank = jnp.dot(cotangent, adapter_down_second.T, preferred_element_type=jnp.float32).astype(jnp.bfloat16)
    hidden_gradient = jnp.dot(cotangent, down_weight.T, preferred_element_type=jnp.float32)
    hidden_gradient = hidden_gradient + adapter_scale * jnp.dot(backward_lowrank, adapter_down_first.T, preferred_element_type=jnp.float32)
    grad_gate = (hidden_gradient * up_values * sigmoid_gate * (1.0 + gate * (1.0 - sigmoid_gate))).astype(jnp.bfloat16)
    grad_up = (hidden_gradient * silu_gate).astype(jnp.bfloat16)
    grad_input = jnp.dot(grad_gate, gate_weight.T, preferred_element_type=jnp.float32)
    grad_input = (grad_input + jnp.dot(grad_up, up_weight.T, preferred_element_type=jnp.float32)).astype(jnp.bfloat16)
    gradient_factor_first = adapter_scale * jnp.dot(hidden_activation.T, backward_lowrank, preferred_element_type=jnp.float32)
    gradient_factor_second = adapter_scale * jnp.dot(lowrank_product.T, cotangent, preferred_element_type=jnp.float32)
    return grad_input, gradient_factor_first, gradient_factor_second
```

```python
import jax
import jax.numpy as jnp
from jax import lax
from jax.sharding import PartitionSpec as P

adapter_scale = 0.5
HIDDEN_CHUNKS = 4
ROW_CHUNKS = 2
GATHER_CHUNKS = 2


def contract_trailing(left, right):
    return lax.dot_general(
        left, right, (((1,), (1,)), ((), ())), preferred_element_type=jnp.float32
    )


def contract_leading(left, right):
    return lax.dot_general(
        left, right, (((0,), (0,)), ((), ())), preferred_element_type=jnp.float32
    )


def low(value):
    return value.astype(jnp.bfloat16)


def wide(value):
    return value.astype(jnp.float32)


def exchange(value, axis, size, bit):
    return lax.ppermute(value, axis, [(i, i ^ (1 << bit)) for i in range(size)])


def solution(mesh):
    pipe, fsdp = mesh.shape["pipe"], mesh.shape["fsdp"]
    pipe_bits, fsdp_bits = pipe.bit_length() - 1, fsdp.bit_length() - 1
    orders = (tuple(range(pipe_bits)), tuple(reversed(range(pipe_bits))))

    def relative_rows(value, me):
        rows, columns = value.shape
        group = rows // (fsdp * pipe * ROW_CHUNKS)
        value = value.reshape(fsdp, pipe, ROW_CHUNKS, group, columns)
        pieces = [
            lax.dynamic_index_in_dim(value, me ^ q, 1, keepdims=False).transpose(1, 0, 2, 3)
            for q in range(pipe)
        ]
        return jnp.stack(pieces).reshape(rows, columns)

    def scatter_sum(value, order, sent_type=jnp.bfloat16):
        rows, columns = value.shape
        value = value.reshape((2,) * pipe_bits + (rows // pipe, columns))
        held = list(reversed(range(pipe_bits)))
        for bit in order:
            axis = held.index(bit)
            held.remove(bit)
            sent = lax.index_in_dim(value, 1, axis, keepdims=False)
            kept = lax.index_in_dim(value, 0, axis, keepdims=False)
            value = kept + wide(exchange(sent.astype(sent_type), "pipe", pipe, bit))
        return value

    def gather_rows(value, order):
        held = []
        for bit in order:
            axis = sum(1 for other in held if other > bit)
            other_side = exchange(value, "pipe", pipe, bit)
            value = jnp.stack([value, other_side], axis)
            held.append(bit)
        return value.reshape(-1, value.shape[-1])

    def sum_over_pipe(value, order):
        for bit in order:
            value = low(value)
            value = wide(value) + wide(exchange(value, "pipe", pipe, bit))
        return value

    def sum_over_fsdp(value):
        for bit in range(fsdp_bits):
            value = value + exchange(value, "fsdp", fsdp, bit)
        return value

    def scatter_over_fsdp(value, position, sent_type):
        lines = fsdp // 2
        core, line = position % 2, position // 2
        blocks = value.shape[0], lines, 2, value.shape[2], value.shape[3]
        value = value.reshape(blocks)
        sent = lax.dynamic_index_in_dim(value, 1 - core, 2, keepdims=False)
        kept = lax.dynamic_index_in_dim(value, core, 2, keepdims=False)
        value = kept + wide(exchange(sent.astype(sent_type), "fsdp", fsdp, 0))
        ring = [(i, (i + 2) % fsdp) for i in range(fsdp)]

        def block(back):
            return lax.dynamic_index_in_dim(
                value, (line + 2 * lines - back) % lines, 1, keepdims=False
            )

        total = block(1)
        for step in range(1, lines):
            arrived = lax.ppermute(total.astype(sent_type), "fsdp", ring)
            total = wide(arrived) + block(step + 1)
        return total

    def shards(tokens, cotangent, gate_weight, up_weight, down_weight, first, second):
        me = lax.axis_index("pipe")
        position = lax.axis_index("fsdp")
        rows = tokens.shape[0]
        hidden = gate_weight.shape[1]
        width = hidden // HIDDEN_CHUNKS
        own = rows // pipe

        cotangent = relative_rows(cotangent, me)
        tokens = relative_rows(tokens, me)
        back_low = low(scatter_sum(contract_trailing(cotangent, second), orders[0], jnp.float32))

        gate_grads, up_grads, activations = [], [], []
        for chunk in range(HIDDEN_CHUNKS):
            cut = slice(chunk * width, (chunk + 1) * width)
            hidden_gradient = contract_trailing(cotangent, down_weight[cut])
            gate = jnp.dot(tokens, gate_weight[:, cut], preferred_element_type=jnp.float32)
            up_values = jnp.dot(tokens, up_weight[:, cut], preferred_element_type=jnp.float32)
            hidden_gradient = scatter_sum(hidden_gradient, orders[chunk % 2])
            gate = scatter_sum(gate, orders[0])
            up_values = scatter_sum(up_values, orders[1])
            hidden_gradient = hidden_gradient + adapter_scale * contract_trailing(
                back_low, first[cut]
            )
            sigmoid_gate = jax.nn.sigmoid(gate)
            silu_gate = gate * sigmoid_gate
            activations.append(low(silu_gate * up_values))
            gate_grads.append(
                low(
                    hidden_gradient
                    * up_values
                    * sigmoid_gate
                    * (1.0 + gate * (1.0 - sigmoid_gate))
                )
            )
            up_grads.append(low(hidden_gradient * silu_gate))
        activation = jnp.concatenate(activations, 1)
        gate_grad = jnp.concatenate(gate_grads, 1)
        up_grad = jnp.concatenate(up_grads, 1)

        part = hidden // GATHER_CHUNKS
        sent_types = [jnp.float32] * (ROW_CHUNKS - 1) + [jnp.bfloat16]
        share = own // ROW_CHUNKS
        inputs = []
        for chunk in range(ROW_CHUNKS):
            picked = slice(chunk * share, (chunk + 1) * share)
            total = 0.0
            for piece in range(GATHER_CHUNKS):
                cut = slice(piece * part, (piece + 1) * part)
                gate_rows = gather_rows(gate_grad[picked, cut], orders[0])
                up_rows = gather_rows(up_grad[picked, cut], orders[1])
                total = total + (
                    contract_trailing(gate_rows, gate_weight[:, cut])
                    + contract_trailing(up_rows, up_weight[:, cut])
                )
            total = total.reshape(pipe, fsdp, share // fsdp, -1)
            inputs.append(low(scatter_over_fsdp(total, position, sent_types[chunk])))
        grad_input = jnp.stack(inputs, 1)
        grad_input = jnp.stack(
            [lax.dynamic_index_in_dim(grad_input, me ^ q, 0, keepdims=False) for q in range(pipe)]
        ).reshape(rows // fsdp, -1)

        grad_first = contract_leading(back_low, activation)
        half = grad_first.shape[0] // 2
        grad_first = jnp.concatenate(
            [
                sum_over_pipe(grad_first[:half], orders[0]),
                sum_over_pipe(grad_first[half:], orders[1]),
            ]
        )
        grad_first = adapter_scale * grad_first.T

        low_rank = low(
            sum_over_fsdp(jnp.dot(activation, first, preferred_element_type=jnp.float32))
        )
        low_rank = gather_rows(low_rank, orders[0])
        grad_second = adapter_scale * contract_leading(low_rank, cotangent)
        return (grad_input, grad_first, grad_second)

    return jax.shard_map(
        shards,
        mesh=mesh,
        in_specs=(
            P(None, "pipe"),
            P(None, "pipe"),
            P("pipe", "fsdp"),
            P("pipe", "fsdp"),
            P("fsdp", "pipe"),
            P("fsdp", None),
            P(None, "pipe"),
        ),
        out_specs=(P("fsdp", "pipe"), P("fsdp", None), P(None, "pipe")),
        check_vma=False,
    )
```

```python
import functools

import jax
import jax.numpy as jnp
from jax import lax
from jax.experimental import pallas as pl
from jax.experimental.pallas import tpu as pltpu
from jax.sharding import PartitionSpec as P

adapter_scale = 0.5
CHUNKS = 7
PIECES = (4, 3)
DEPTH = 768
VMEM_LIMIT = 56 * 1024 * 1024


def contract_trailing(left, right):
    return lax.dot_general(
        left, right, (((1,), (1,)), ((), ())), preferred_element_type=jnp.float32
    )


def contract_leading(left, right):
    return lax.dot_general(
        left, right, (((0,), (0,)), ((), ())), preferred_element_type=jnp.float32
    )


def low(value):
    return value.astype(jnp.bfloat16)


def wide(value):
    return value.astype(jnp.float32)


def exchange(value, axis, size, bit):
    return lax.ppermute(value, axis, [(i, i ^ (1 << bit)) for i in range(size)])


def shape_of(shape, dtype):
    return jax.ShapeDtypeStruct(shape, dtype)


def gradients(hidden_gradient, gate, up_values):
    sigmoid_gate = jax.nn.sigmoid(gate)
    silu_gate = gate * sigmoid_gate
    activation = silu_gate * up_values
    grad_gate = (
        hidden_gradient * up_values * sigmoid_gate * (1.0 + gate * (1.0 - sigmoid_gate))
    )
    return low(grad_gate), low(hidden_gradient * silu_gate), low(activation)


def grad_input_kernel(steps, width, has_base, *refs):
    gate_rows, up_rows, gate_weight, up_weight = refs[:4]
    base = refs[4] if has_base else None
    out, total = refs[-2:]
    step = pl.program_id(1)
    columns = pl.ds(pl.multiple_of(step * width, width), width)
    part = contract_trailing(gate_rows[:, columns], gate_weight[...]) + contract_trailing(
        up_rows[:, columns], up_weight[...]
    )

    @pl.when(step == 0)
    def _():
        total[...] = part + base[...] if has_base else part

    @pl.when(step > 0)
    def _():
        total[...] += part

    @pl.when(step == steps - 1)
    def _():
        out[...] = total[...]


def grad_input_part(gate_rows, up_rows, gate_weight, up_weight, first_chunk, width, base):
    rows, part = gate_rows.shape
    features = gate_weight.shape[0]
    steps = part // width
    weight = pl.BlockSpec((DEPTH, width), lambda j, c: (j, first_chunk + c))
    whole = pl.BlockSpec((rows, part), lambda j, c: (0, 0))
    block = pl.BlockSpec((rows, DEPTH), lambda j, c: (0, j))
    operands = [gate_rows, up_rows, gate_weight, up_weight]
    specs = [whole, whole, weight, weight]
    if base is not None:
        operands.append(base)
        specs.append(block)
    return pl.pallas_call(
        functools.partial(grad_input_kernel, steps, width, base is not None),
        grid=(features // DEPTH, steps),
        in_specs=specs,
        out_specs=block,
        out_shape=shape_of((rows, features), jnp.float32),
        scratch_shapes=[pltpu.VMEM((rows, DEPTH), jnp.float32)],
        compiler_params=pltpu.CompilerParams(vmem_limit_bytes=VMEM_LIMIT),
        cost_estimate=pl.CostEstimate(
            flops=4 * rows * part * features,
            bytes_accessed=4 * part * features + 4 * rows * features,
            transcendentals=0,
        ),
    )(*operands)


class Stages:
    def __init__(self, pipe, rows, hidden, contraction):
        self.pipe = pipe
        self.bits = pipe.bit_length() - 1
        self.half = rows // 2
        self.width = hidden // CHUNKS
        self.grid = contraction // DEPTH
        self.orders = (tuple(range(self.bits)), tuple(reversed(range(self.bits))))

    def live(self, stage, step):
        return 0 <= stage - 2 * step < CHUNKS

    def sent_rows(self, step):
        return self.half >> (step + 1)

    def parts(self, stage, bit):
        steps = [(h, self.orders[h].index(bit)) for h in (0, 1)]
        steps.sort(key=lambda item: item[1])
        found, at = [], 0
        for h, step in steps:
            if self.live(stage, step):
                found.append((h, step, at, self.sent_rows(step)))
                at += self.sent_rows(step)
        return found, at

    def call(self, stage, tokens, cotangent, weights, back_low, first, received, kept):
        bits, width, grid, half = self.bits, self.width, self.grid, self.half
        columns = 3 * width
        operands, specs, names = [], [], []
        out_shapes, out_specs, out_names = [], [], []

        def take(name, value, block, index):
            names.append(name)
            operands.append(value)
            specs.append(pl.BlockSpec(block, index))

        def give(name, shape, dtype, block, index):
            out_names.append(name)
            out_shapes.append(shape_of(shape, dtype))
            out_specs.append(pl.BlockSpec(block, index))

        multiply = self.live(stage, 0)
        last = self.live(stage, bits)
        if multiply:
            rows = 2 * half
            take("tokens", tokens, (rows, DEPTH), lambda k: (0, k))
            take("cotangent", cotangent, (rows, DEPTH), lambda k: (0, k))
            take("gate", weights[0], (DEPTH, width), lambda k: (k, stage))
            take("up", weights[1], (DEPTH, width), lambda k: (k, stage))
            take("down", weights[2], (width, DEPTH), lambda k: (stage, k))
        for step in range(1, bits + 1):
            if not self.live(stage, step):
                continue
            rows = half >> step
            block = rows // grid
            take(
                ("kept", step), kept[step - 1], (2, block, columns), lambda k: (0, k, 0)
            )
            for h in (0, 1):
                bit = self.orders[h][step - 1]
                at = next(
                    part[2] for part in self.parts(stage - 2, bit)[0] if part[0] == h
                )
                take(
                    ("received", step, h),
                    received[bit],
                    (block, columns),
                    functools.partial(lambda base, k: (base + k, 0), at // block),
                )
        if last:
            block = (half >> bits) // grid
            chunk = stage - 2 * bits
            take("back_low", back_low, (2, block, back_low.shape[2]), lambda k: (0, k, 0))
            take("first", first, (width, first.shape[1]), lambda k: (chunk, 0))
            for name in ("grad_gate", "grad_up", "activation"):
                give(
                    name,
                    (2, half >> bits, width),
                    jnp.bfloat16,
                    (2, block, width),
                    lambda k: (0, k, 0),
                )
        for step in range(bits):
            if self.live(stage, step):
                rows = self.sent_rows(step)
                give(
                    ("kept", step),
                    (2, rows, columns),
                    jnp.float32,
                    (2, rows, columns),
                    lambda k: (0, 0, 0),
                )
        for bit in range(bits):
            rows = self.parts(stage, bit)[1]
            if rows:
                give(
                    ("sent", bit),
                    (rows, columns),
                    jnp.bfloat16,
                    (rows, columns),
                    lambda k: (0, 0),
                )

        def kernel(*refs):
            into = dict(zip(names, refs))
            out = dict(zip(out_names, refs[len(names) :]))
            k = pl.program_id(0)

            def slot(h, step):
                bit = self.orders[h][step]
                at = next(part[2] for part in self.parts(stage, bit)[0] if part[0] == h)
                return out[("sent", bit)], at

            for step in range(1, bits + 1):
                if not self.live(stage, step):
                    continue
                rows = half >> step
                block = rows // grid
                sums = [
                    into[("kept", step)][h] + wide(into[("received", step, h)][...])
                    for h in (0, 1)
                ]
                if step < bits:
                    keep = rows // 2
                    at = k * block

                    @pl.when(at < keep)
                    def _():
                        for h in (0, 1):
                            out[("kept", step)][h, pl.ds(pl.multiple_of(at, block), block), :] = (
                                sums[h]
                            )

                    @pl.when(at >= keep)
                    def _():
                        for h in (0, 1):
                            ref, start = slot(h, step)
                            place = pl.multiple_of(start + at - keep, block)
                            ref[pl.ds(place, block), :] = low(sums[h])
                else:
                    for h in (0, 1):
                        hidden_gradient = sums[h][:, 2 * width :] + adapter_scale * contract_trailing(
                            into["back_low"][h], into["first"][...]
                        )
                        values = gradients(
                            hidden_gradient, sums[h][:, :width], sums[h][:, width : 2 * width]
                        )
                        for name, value in zip(("grad_gate", "grad_up", "activation"), values):
                            out[name][h] = value
            if multiply:
                total = refs[-1]
                products = (
                    jnp.dot(
                        into["tokens"][...], into["gate"][...], preferred_element_type=jnp.float32
                    ),
                    jnp.dot(
                        into["tokens"][...], into["up"][...], preferred_element_type=jnp.float32
                    ),
                    contract_trailing(into["cotangent"][...], into["down"][...]),
                )
                for unit, product in enumerate(products):
                    cut = slice(unit * width, (unit + 1) * width)

                    @pl.when(k == 0)
                    def _():
                        total[:, cut] = product

                    @pl.when(k > 0)
                    def _():
                        total[:, cut] += product

                @pl.when(k == grid - 1)
                def _():
                    rows = half // 2
                    for h in (0, 1):
                        out[("kept", 0)][h] = total[h * half : h * half + rows, :]
                        ref, start = slot(h, 0)
                        ref[start : start + rows, :] = low(
                            total[h * half + rows : (h + 1) * half, :]
                        )

        scratch = [pltpu.VMEM((2 * half, columns), jnp.float32)] if multiply else []
        contraction = grid * DEPTH
        flops = 2 * 2 * half * contraction * columns if multiply else 0
        moved = 2 * contraction * columns + 8 * half * contraction if multiply else 0
        results = pl.pallas_call(
            kernel,
            grid=(grid,),
            in_specs=specs,
            out_specs=out_specs,
            out_shape=out_shapes,
            scratch_shapes=scratch,
            compiler_params=pltpu.CompilerParams(vmem_limit_bytes=VMEM_LIMIT),
            cost_estimate=pl.CostEstimate(
                flops=flops,
                bytes_accessed=moved + 2 * half * columns * 4,
                transcendentals=0,
            ),
        )(*operands)
        return dict(zip(out_names, results))


def solution(mesh):
    pipe, fsdp = mesh.shape["pipe"], mesh.shape["fsdp"]
    pipe_bits, fsdp_bits = pipe.bit_length() - 1, fsdp.bit_length() - 1
    orders = (tuple(range(pipe_bits)), tuple(reversed(range(pipe_bits))))
    places = [
        [
            sum(((i >> (pipe_bits - 1 - j)) & 1) << bit for j, bit in enumerate(order))
            for i in range(pipe)
        ]
        for order in orders
    ]

    def relative_rows(value, me):
        rows, columns = value.shape
        group = rows // (fsdp * pipe * 2)
        value = value.reshape(fsdp, pipe, 2, group, columns)
        pieces = [
            lax.dynamic_index_in_dim(value[:, :, h], me ^ q, 1, keepdims=False)
            for h in (0, 1)
            for q in places[h]
        ]
        return jnp.stack(pieces).reshape(rows, columns)

    def scatter_sum(value):
        for bit in reversed(range(pipe_bits)):
            value = value.reshape(2, -1, *value.shape[1:])
            value = value[0] + exchange(value[1], "pipe", pipe, bit)
        return value[0]

    def gather_rows(value, order):
        held = []
        for bit in order:
            axis = sum(1 for other in held if other > bit)
            other_side = exchange(value, "pipe", pipe, bit)
            value = jnp.stack([value, other_side], axis)
            held.append(bit)
        return value.reshape(-1, value.shape[-1])

    def sum_over_pipe(value, order):
        for bit in order:
            value = low(value)
            value = wide(value) + wide(exchange(value, "pipe", pipe, bit))
        return value

    def sum_over_fsdp(value):
        for bit in range(fsdp_bits):
            value = value + exchange(value, "fsdp", fsdp, bit)
        return value

    def scatter_over_fsdp(value, position, sent_type):
        lines = fsdp // 2
        core, line = position % 2, position // 2
        blocks = value.shape[0], lines, 2, value.shape[2], value.shape[3]
        value = value.reshape(blocks)
        sent = lax.dynamic_index_in_dim(value, 1 - core, 2, keepdims=False)
        kept = lax.dynamic_index_in_dim(value, core, 2, keepdims=False)
        value = kept + wide(exchange(sent.astype(sent_type), "fsdp", fsdp, 0))
        ring = [(i, (i + 2) % fsdp) for i in range(fsdp)]

        def block(back):
            return lax.dynamic_index_in_dim(
                value, (line + 2 * lines - back) % lines, 1, keepdims=False
            )

        total = block(1)
        for step in range(1, lines):
            arrived = lax.ppermute(total.astype(sent_type), "fsdp", ring)
            total = wide(arrived) + block(step + 1)
        return total

    def shards(tokens, cotangent, gate_weight, up_weight, down_weight, first, second):
        me = lax.axis_index("pipe")
        position = lax.axis_index("fsdp")
        rows = tokens.shape[0]
        contraction, hidden = gate_weight.shape
        stages = Stages(pipe, rows, hidden, contraction)
        width = stages.width
        share = rows // (2 * pipe)

        cotangent = relative_rows(cotangent, me)
        tokens = relative_rows(tokens, me)
        back_low = contract_trailing(cotangent, second).reshape(2, pipe, share, -1)
        back_low = jnp.stack(
            [
                jnp.stack([back_low[h, places[h].index(q)] for h in (0, 1)])
                for q in range(pipe)
            ]
        )
        back_low = low(scatter_sum(back_low))

        weights = (gate_weight, up_weight, down_weight)
        results, arrived, finished = [], [], []
        for stage in range(CHUNKS + 2 * pipe_bits):
            old = results[stage - 2] if stage >= 2 else {}
            result = stages.call(
                stage,
                tokens,
                cotangent,
                weights,
                back_low,
                first,
                arrived[stage - 2] if stage >= 2 else {},
                {step: old.get(("kept", step)) for step in range(pipe_bits)},
            )
            results.append(result)
            arrived.append(
                {
                    bit: exchange(result[("sent", bit)], "pipe", pipe, bit)
                    for bit in range(pipe_bits)
                    if ("sent", bit) in result
                }
            )
            if "grad_gate" in result:
                finished.append(result)

        inputs = []
        sent_types = (jnp.float32, jnp.bfloat16)
        for h in (0, 1):
            total, at = None, 0
            for count in PIECES:
                picked = finished[at : at + count]
                gate_rows = gather_rows(
                    jnp.concatenate([item["grad_gate"][h] for item in picked], 1), orders[0]
                )
                up_rows = gather_rows(
                    jnp.concatenate([item["grad_up"][h] for item in picked], 1), orders[1]
                )
                total = grad_input_part(
                    gate_rows, up_rows, gate_weight, up_weight, at, width, total
                )
                at += count
            total = total.reshape(pipe, fsdp, share // fsdp, -1)
            inputs.append(low(scatter_over_fsdp(total, position, sent_types[h])))
        grad_input = jnp.stack(inputs, 1)
        grad_input = jnp.stack(
            [lax.dynamic_index_in_dim(grad_input, me ^ q, 0, keepdims=False) for q in range(pipe)]
        ).reshape(rows // fsdp, -1)

        activation = jnp.concatenate([item["activation"] for item in finished], 2)
        activation = activation.reshape(2 * share, hidden)
        grad_first = contract_leading(back_low.reshape(2 * share, -1), activation)
        cut = grad_first.shape[0] // 2
        grad_first = jnp.concatenate(
            [
                sum_over_pipe(grad_first[:cut], orders[0]),
                sum_over_pipe(grad_first[cut:], orders[1]),
            ]
        )
        grad_first = adapter_scale * grad_first.T

        low_rank = low(
            sum_over_fsdp(jnp.dot(activation, first, preferred_element_type=jnp.float32))
        )
        low_rank = gather_rows(low_rank, orders[0]).reshape(pipe, 2, share, -1)
        low_rank = jnp.stack([low_rank[q, h] for h in (0, 1) for q in places[h]])
        grad_second = adapter_scale * contract_leading(low_rank.reshape(rows, -1), cotangent)
        return (grad_input, grad_first, grad_second)

    return jax.shard_map(
        shards,
        mesh=mesh,
        in_specs=(
            P(None, "pipe"),
            P(None, "pipe"),
            P("pipe", "fsdp"),
            P("pipe", "fsdp"),
            P("fsdp", "pipe"),
            P("fsdp", None),
            P(None, "pipe"),
        ),
        out_specs=(P("fsdp", "pipe"), P("fsdp", None), P(None, "pipe")),
        check_vma=False,
    )
```
